32 devices in a mesh: dom: 8 (over z, y), grp: 4 (over x, core).
Axes of the slice: x: 2, y: 2, z: 4, core: 2. Of those that a mesh axis runs over, the one named last changes fastest.
Arguments:
- residual_in: bfloat16 [256, 32, 625], P(('dom', 'grp')), may hold values from -6 to 6
- block_inverse: bfloat16 [256, 625, 625], P(('dom', 'grp')), may hold values from -0.25 to 0.25
- coupling: bfloat16 [512, 625, 625], P(('dom', 'grp')), may hold values from -0.25 to 0.25
- tile_region: int32 [512, 1], P(('dom', 'grp')), may hold values from 0 to 7; in each aligned block of 16 rows (0 to 15, 16 to 31, ...) at most 2 rows name the same one
- tile_source: int32 [512], P(('dom', 'grp')), may hold values from 0 to 7
- tile_target: int32 [512], P(('dom', 'grp')), may hold values from 0 to 7
- interface_basis: bfloat16 [256, 625, 64], P(('dom', 'grp')), may hold values from -0.25 to 0.25
- reduced_inverse: float32 [8, 64, 64], P('dom'), may hold values from -0.75 to 0.75
Outputs:
- preconditioned: float32 [256, 32, 625], P(('dom', 'grp'))
The draws below stay inside these ranges and needn't reach their ends.
Inputs may be any that keep to these rules, and one draw needn't show every extreme that they name: `tile_region`: among the 16 tiles of one device, at most 2 name the same region; in every draw some device names some region exactly 2 times.
All inputs are finite; a program needn't handle non-finite values.
Results may differ from the reference program's by a relative error of at most 0.013.
Values may be sent and summed in bfloat16 or wider, within the bound.
A program may use at most 256 MiB of HBM per device.

```python
import math
import jax
import jax.numpy as jnp
import numpy as np
from jax import lax

B = 625
K = 32
M = 64
CAP = 2
EL = 8
TL = 16
E_TOT = 256
TILES = 512
N_DOM = 8
N_GRP = 4


def plant(result, own_key, low, high):
    shape = result.shape
    index_at = [jax.random.randint(jax.random.fold_in(own_key, axis), (), 0, shape[axis]) for axis in range(len(shape))]
    result = result.at[tuple(index_at)].set(low)
    longest = shape.index(max(shape))
    index_at[longest] = (index_at[longest] + 1) % shape[longest]
    return result.at[tuple(index_at)].set(high)


def block_levels(stream_key, extent, pieces, smallest, top_value):
    level, own = 1.0, jax.random.fold_in(stream_key, 6)
    for position, blocks in pieces:
        draws = jnp.exp(jax.random.uniform(jax.random.fold_in(own, position), (blocks,), jnp.float32, smallest / len(pieces), top_value / len(pieces)))
        level = level * jnp.repeat(draws, extent[position] // blocks).reshape([-1 if axis == position else 1 for axis in range(len(extent))])
    return level


def assign_block(rng, own, number, rows, number_of, top, most, skew):
    order = jax.random.permutation(rng, number_of)
    crowded, usual = shares(number_of, rows * top, most, skew, True), shares(number_of, rows * top, most, skew, False)
    places = jnp.arange(number_of)

    def named(tallies, rotation):
        used = int((tallies > 0).sum())
        fixed = max(1, used // 4)
        moved = fixed + (places - fixed + rotation * (used - fixed)) % max(1, number_of - fixed)
        return jnp.zeros((number_of,), jnp.int32).at[order[jnp.where(places < fixed, places, moved)]].set(jnp.asarray(tallies, jnp.int32))

    tallies = jnp.where(number % 4 == 0, named(crowded, number // 4), named(usual, number - number // 4 - 1))
    mixed = jax.random.permutation(jax.random.fold_in(own, 3), number_of)
    source_of, taker = mixed[0:number_of // 2 * 2:2], mixed[1:number_of // 2 * 2:2]
    margin = jnp.minimum(tallies[source_of] - 1, most - tallies[taker]) // 2
    margin = jnp.where((source_of == order[0]) | (taker == order[0]) | (tallies[taker] == 0), 0, jnp.maximum(margin, 0))
    moved = jax.random.randint(jax.random.fold_in(own, 4), (number_of // 2,), 0, 1 << 20) % (margin + 1)
    tallies = tallies.at[source_of].add(-moved).at[taker].add(moved)
    labels = jnp.searchsorted(jnp.cumsum(tallies), jnp.arange(rows * top), side="right").astype(jnp.int32)
    grid = labels.reshape(top, rows).T
    grid = grid[jax.random.permutation(jax.random.fold_in(own, 1), rows)]
    rotation = jax.random.randint(jax.random.fold_in(own, 2), (rows, 1), 0, top)
    return jnp.take_along_axis(grid, (jnp.arange(top)[None, :] + rotation) % top, axis=1)


def shares(number_of, total, bound, skew, full):
    loads = [(1 << 20) // math.isqrt(standing ** skew) + 1 for standing in range(1, number_of + 1)]
    largest = bound if full else min(bound, max(-(-total // number_of), total * loads[0] // sum(loads)))
    least = 1 if total - largest >= number_of - 1 else 0
    given, surplus = [largest] + [least] * (number_of - 1), total - largest - least * (number_of - 1)
    while surplus > 0:
        movable = [i for i in range(1, number_of) if given[i] < largest] or [i for i in range(1, number_of) if given[i] < bound]
        pool, left = sum([loads[i] for i in movable]), surplus
        for i in movable:
            extra = min(bound - given[i], max(1, left * loads[i] // pool), surplus)
            given[i] = given[i] + extra
            surplus = surplus - extra
    return np.array(given)


def scatter_about(own_key, extent, scale, reach, shards=(), held_as=jnp.bfloat16):
    array = jax.random.normal(own_key, extent, jnp.float32) * scale
    if len(shards) > 0:
        array = block_levels(own_key, extent, shards, -0.22, 0.18) * array
    return jnp.clip(array, min=-reach, max=reach).astype(held_as)


def setup_inputs(seed: int = 0) -> dict:
    key_of = jax.random.split(jax.random.key(seed), 9)
    residual_in = scatter_about(key_of[0], (E_TOT, K, B), 1.0, 6.0, ((0, 32),))
    block_inverse = scatter_about(key_of[1], (E_TOT, B, B), B ** -0.5, 0.25, ((0, 32),))
    coupling = scatter_about(key_of[2], (TILES, B, B), B ** -0.5, 0.25, ((0, 32),))
    tile_region_keys = jax.random.split(jax.random.fold_in(key_of[3], 1), TILES // TL)
    tile_region_turns = jax.random.permutation(jax.random.fold_in(key_of[3], 3), TILES // TL)
    tile_region = jax.vmap(lambda own, number: assign_block(jax.random.fold_in(key_of[3], 2), own, number, TL, N_DOM, 1, CAP, 2))(tile_region_keys, tile_region_turns).reshape((TILES, 1))
    tile_source = plant(jax.random.randint(key_of[4], (TILES,), 0, EL), jax.random.fold_in(key_of[4], 1), 0, EL - 1).astype(jnp.int32)
    tile_target = plant(jax.random.randint(key_of[5], (TILES,), 0, EL), jax.random.fold_in(key_of[5], 1), 0, EL - 1).astype(jnp.int32)
    interface_basis = scatter_about(key_of[6], (E_TOT, B, M), B ** -0.5, 0.25, ((0, 32),))
    reduced_inverse = scatter_about(key_of[7], (N_DOM, M, M), M ** -0.5, 0.75, ((0, 8),), jnp.float32)
    return dict(residual_in=residual_in, block_inverse=block_inverse, coupling=coupling, tile_region=tile_region, tile_source=tile_source, tile_target=tile_target, interface_basis=interface_basis, reduced_inverse=reduced_inverse)


def apply_blocks(values, blocks):
    return lax.map(lambda pair: jnp.dot(pair[0], pair[1], preferred_element_type=jnp.float32), (values, blocks))


def reference(residual_in, block_inverse, coupling, tile_region, tile_source, tile_target, interface_basis, reduced_inverse):
    e_total = residual_in.shape[0]
    t_total = coupling.shape[0]
    initial = apply_blocks(residual_in, block_inverse).astype(jnp.bfloat16)
    owner = (jnp.arange(t_total, dtype=jnp.int32) // TL).astype(jnp.int32)
    source_global = owner * EL + tile_source
    target_dev = tile_region[:, 0] * N_GRP + owner % N_GRP
    target_global = (target_dev * EL + tile_target).astype(jnp.int32)
    gathered = initial[source_global]
    products = apply_blocks(gathered, coupling)
    coupled = jax.ops.segment_sum(products, target_global, num_segments=e_total)
    corrected_in = (residual_in.astype(jnp.float32) - coupled).astype(jnp.bfloat16)
    second = apply_blocks(corrected_in, block_inverse)
    second_b = second.astype(jnp.bfloat16)
    per_element = apply_blocks(second_b, interface_basis)
    reduced = per_element.reshape(N_DOM, N_GRP * EL, K, M).sum(axis=1)
    solved = jnp.einsum("rkm,rmn->rkn", reduced, reduced_inverse, precision=lax.Precision.HIGHEST).astype(jnp.bfloat16)
    spread = jnp.repeat(solved, N_GRP * EL, axis=0)
    correction = lax.map(lambda pair: jnp.dot(pair[0], pair[1].T, preferred_element_type=jnp.float32), (spread, interface_basis))
    return second + correction
```

```python
import functools

import jax
import jax.numpy as jnp
from jax import lax
from jax.experimental import pallas as pl
from jax.experimental.pallas import tpu as pltpu
from jax.sharding import PartitionSpec as P

CAP = 2
F32 = jnp.float32
BF16 = jnp.bfloat16


def partner(me, offset, count):
    other, bit = 0, 1
    while bit < count:
        other = other + ((me // bit + offset // bit) % 2) * bit
        bit *= 2
    return other


def spread_apply(rows, spread, weights, total, ready):
    height, width = rows.shape
    blocks = weights.shape[1]
    step = spread.shape[0]
    depth = height // blocks
    for start in range(0, width, step):
        size = min(step, width - start)
        wide = jnp.dot(
            rows[:, start : start + size],
            spread[:size, : size * blocks],
            preferred_element_type=F32,
        )
        row = lax.broadcasted_iota(jnp.int32, wide.shape, 0) // depth
        column = lax.broadcasted_iota(jnp.int32, wide.shape, 1) % blocks
        wide = jnp.where(row == column, wide, 0.0).astype(BF16)
        ready(start // step)
        block = weights[start : start + size].reshape(size * blocks, width)
        part = jnp.dot(wide, block, preferred_element_type=F32)
        if start == 0:
            total[...] = part
        else:
            total[...] += part


def kernel(
    regions,
    groups,
    region_ref,
    source_ref,
    target_ref,
    residual_hbm,
    binv_hbm,
    coupling_hbm,
    basis_hbm,
    rinv_hbm,
    out_hbm,
    binv,
    coupling,
    basis,
    basis_t,
    residual,
    rinv,
    initial,
    gathered,
    products,
    corrected,
    spread,
    total,
    acc,
    second,
    send,
    recv,
    meta_send,
    meta_recv,
    red_send,
    red_recv,
    perm,
    meta_smem,
    load_sem,
    binv_sem,
    coupling_sem,
    out_sem,
    send_sem,
    recv_sem,
    meta_send_sem,
    meta_recv_sem,
    meta_local_sem,
    red_send_sem,
    red_recv_sem,
):
    dom, grp = lax.axis_index("dom"), lax.axis_index("grp")
    elements, vectors, width = initial.shape
    tiles = products.shape[0]
    parts, blocks = coupling.shape[0], coupling.shape[2]
    modes = basis_t.shape[1]
    step = spread.shape[0]
    starts = list(range(0, width, step))
    half = regions // 2

    load_residual = pltpu.make_async_copy(residual_hbm, residual, load_sem.at[0])
    load_basis = pltpu.make_async_copy(basis_hbm, basis_t, load_sem.at[1])
    load_rinv = pltpu.make_async_copy(rinv_hbm.at[0], rinv, load_sem.at[2])

    def load_binv(i):
        rows = pl.ds(starts[i], min(step, width - starts[i]))
        return pltpu.make_async_copy(binv_hbm.at[rows], binv.at[rows], binv_sem.at[i])

    def load_coupling(h, i):
        rows = pl.ds(starts[i], min(step, width - starts[i]))
        return pltpu.make_async_copy(
            coupling_hbm.at[rows, h], coupling.at[h, rows], coupling_sem.at[h, i]
        )

    load_residual.start()
    for i in range(len(starts)):
        load_binv(i).start()
    for h in range(parts):
        for i in range(len(starts)):
            load_coupling(h, i).start()
    load_basis.start()
    load_rinv.start()

    barrier = pltpu.get_barrier_semaphore()
    for k in range(1, regions):
        pl.semaphore_signal(barrier, inc=1, device_id=(partner(dom, k, regions), grp))
    for j in range(1, groups):
        pl.semaphore_signal(barrier, inc=1, device_id=(dom, partner(grp, j, groups)))

    row = lax.broadcasted_iota(jnp.int32, spread.shape, 0)
    column = lax.broadcasted_iota(jnp.int32, spread.shape, 1) // blocks
    spread[...] = jnp.where(row == column, 1.0, 0.0).astype(BF16)

    named = [region_ref[t] for t in range(tiles)]
    for k in range(regions):
        place = partner(dom, k, regions)
        first, last = jnp.int32(tiles), jnp.int32(-1)
        for t in range(tiles):
            last = jnp.where(named[t] == place, t, last)
            first = jnp.where(named[tiles - 1 - t] == place, tiles - 1 - t, first)
        has_first = last >= 0
        has_last = last > first
        first = jnp.where(has_first, first, 0)
        last = jnp.where(has_last, last, 0)
        perm[CAP * k] = first
        perm[CAP * k + 1] = last
        aim_first = jnp.where(has_first, target_ref[first], -1)
        aim_last = jnp.where(has_last, target_ref[last], -1)
        meta_send[k, 0:1, :] = jnp.full((1, 128), aim_first, jnp.int32)
        meta_send[k, 1:2, :] = jnp.full((1, 128), aim_last, jnp.int32)

    load_residual.wait()

    def rows_of(e):
        return pl.ds(e * vectors, vectors)

    spread_apply(residual, spread, binv, total, lambda i: load_binv(i).wait())
    for e in range(elements):
        initial[e] = total[rows_of(e)].astype(BF16)

    for t in range(tiles):
        gathered[rows_of(t)] = initial[source_ref[t]]
    for h in range(parts):
        spread_apply(
            gathered.at[pl.ds(h * blocks * vectors, blocks * vectors)],
            spread,
            coupling.at[h],
            total,
            lambda i, h=h: load_coupling(h, i).wait(),
        )
        for i in range(blocks):
            products[h * blocks + i] = total[rows_of(i)].astype(BF16)

    def meta_copy(k):
        return pltpu.make_async_remote_copy(
            src_ref=meta_send.at[k],
            dst_ref=meta_recv.at[k],
            send_sem=meta_send_sem.at[k],
            recv_sem=meta_recv_sem.at[k],
            device_id=(partner(dom, k, regions), grp),
        )

    def product_copy(k, c):
        s = CAP * k + c
        return pltpu.make_async_remote_copy(
            src_ref=send.at[s],
            dst_ref=recv.at[s],
            send_sem=send_sem.at[s],
            recv_sem=recv_sem.at[s],
            device_id=(partner(dom, k, regions), grp),
        )

    pl.semaphore_wait(barrier, regions - 1 + groups - 1)
    for k in range(1, regions):
        meta_copy(k).start()

    def send_products(i, carry):
        k = regions - 1 - i
        for c in range(CAP):
            send[CAP * k + c] = products[perm[CAP * k + c]]
            product_copy(k, c).start()
        return carry

    lax.fori_loop(0, regions - 1, send_products, 0)
    meta_recv[0] = meta_send[0]
    for c in range(CAP):
        recv[c] = products[perm[c]]

    load_basis.wait()
    load_rinv.wait()
    for e in range(elements):
        basis[e] = jnp.swapaxes(basis_t[e].astype(F32), 0, 1).astype(BF16)
        acc[e] = residual[e * vectors : (e + 1) * vectors].astype(F32)
    for k in range(1, regions):
        meta_copy(k).wait()
    meta_local = pltpu.make_async_copy(meta_recv, meta_smem, meta_local_sem.at[0])
    meta_local.start()
    meta_local.wait()

    def weight(k, c, e):
        return jnp.where(meta_smem[k, c, 0] == e, 1.0, 0.0).astype(F32)

    def remaining(k, e, left, right):
        return acc[e] - (weight(k, 0, e) * left + weight(k, 1, e) * right)

    def absorb(k):
        left = recv[CAP * k].astype(F32)
        right = recv[CAP * k + 1].astype(F32)
        for e in range(elements):
            acc[e] = remaining(k, e, left, right)

    def arrive(k):
        for c in range(CAP):
            product_copy(k, c).wait_recv()
        absorb(k)

    def near(i, carry):
        arrive(i + 1)
        return carry

    def far(i, carry):
        arrive(regions - 1 - i)
        return carry

    absorb(0)
    lax.fori_loop(0, half - 1, near, 0)
    lax.fori_loop(0, half - 1, far, 0)
    for c in range(CAP):
        product_copy(half, c).wait_recv()
    left = recv[CAP * half].astype(F32)
    right = recv[CAP * half + 1].astype(F32)
    for e in range(elements):
        corrected[e * vectors : (e + 1) * vectors] = remaining(half, e, left, right).astype(BF16)

    spread_apply(corrected, spread, binv, total, lambda i: None)
    reduced = jnp.zeros((vectors, modes), F32)
    for e in range(elements):
        reduced = reduced + jnp.dot(
            total[rows_of(e)].astype(BF16), basis[e], preferred_element_type=F32
        )
    red_send[...] = reduced

    def red_copy(j):
        return pltpu.make_async_remote_copy(
            src_ref=red_send,
            dst_ref=red_recv.at[j - 1],
            send_sem=red_send_sem.at[j - 1],
            recv_sem=red_recv_sem.at[j - 1],
            device_id=(dom, partner(grp, j, groups)),
        )

    for j in range(1, groups):
        red_copy(j).start()
    for j in range(1, groups):
        red_copy(j).wait()
        reduced = reduced + red_recv[j - 1]
    solved = jnp.dot(
        reduced, rinv[...], precision=lax.Precision.HIGHEST, preferred_element_type=F32
    ).astype(BF16)

    def store(e):
        return pltpu.make_async_copy(second.at[e], out_hbm.at[e], out_sem.at[e])

    for e in range(elements):
        second[e] = total[rows_of(e)] + jnp.dot(solved, basis_t[e], preferred_element_type=F32)
        store(e).start()
    for k in range(1, regions):
        for c in range(CAP):
            product_copy(k, c).wait_send()
    for e in range(elements):
        store(e).wait()


def shards(
    residual_in,
    block_inverse,
    coupling,
    tile_region,
    tile_source,
    tile_target,
    interface_basis,
    reduced_inverse,
):
    regions, groups = lax.axis_size("dom"), lax.axis_size("grp")
    elements, vectors, width = residual_in.shape
    tiles = coupling.shape[0]
    modes = interface_basis.shape[2]
    slots = regions * CAP
    parts = tiles // elements
    step = 128
    chunks = -(-width // step)
    smem = pl.BlockSpec(memory_space=pltpu.SMEM)
    hbm = pl.BlockSpec(memory_space=pl.ANY)
    dma = pltpu.SemaphoreType.DMA
    return pl.pallas_call(
        functools.partial(kernel, regions, groups),
        out_shape=jax.ShapeDtypeStruct((elements, vectors, width), F32),
        in_specs=[smem] * 3 + [hbm] * 5,
        out_specs=hbm,
        scratch_shapes=[
            pltpu.VMEM((width, elements, width), BF16),
            pltpu.VMEM((parts, width, elements, width), BF16),
            pltpu.VMEM((elements, width, modes), BF16),
            pltpu.VMEM((elements, modes, width), BF16),
            pltpu.VMEM((elements * vectors, width), BF16),
            pltpu.VMEM((modes, modes), F32),
            pltpu.VMEM((elements, vectors, width), BF16),
            pltpu.VMEM((tiles * vectors, width), BF16),
            pltpu.VMEM((tiles, vectors, width), BF16),
            pltpu.VMEM((elements * vectors, width), BF16),
            pltpu.VMEM((step, step * elements), BF16),
            pltpu.VMEM((elements * vectors, width), F32),
            pltpu.VMEM((elements, vectors, width), F32),
            pltpu.VMEM((elements, vectors, width), F32),
            pltpu.VMEM((slots, vectors, width), BF16),
            pltpu.VMEM((slots, vectors, width), BF16),
            pltpu.VMEM((regions, 8, 128), jnp.int32),
            pltpu.VMEM((regions, 8, 128), jnp.int32),
            pltpu.VMEM((vectors, modes), F32),
            pltpu.VMEM((groups - 1, vectors, modes), F32),
            pltpu.SMEM((slots,), jnp.int32),
            pltpu.SMEM((regions, 8, 128), jnp.int32),
            dma((3,)),
            dma((chunks,)),
            dma((parts, chunks)),
            dma((elements,)),
            dma((slots,)),
            dma((slots,)),
            dma((regions,)),
            dma((regions,)),
            dma((1,)),
            dma((groups - 1,)),
            dma((groups - 1,)),
        ],
        compiler_params=pltpu.CompilerParams(
            collective_id=0, has_side_effects=True, vmem_limit_bytes=56 * 1024 * 1024
        ),
        cost_estimate=pl.CostEstimate(
            flops=2 * vectors * width * width * (2 * elements + tiles),
            bytes_accessed=2 * width * width * (elements + tiles),
            transcendentals=0,
        ),
    )(
        tile_region[:, 0],
        tile_source,
        tile_target,
        residual_in.reshape(elements * vectors, width),
        jnp.transpose(block_inverse, (1, 0, 2)),
        jnp.transpose(coupling, (1, 0, 2)).reshape(width, parts, elements, width),
        jnp.swapaxes(interface_basis, 1, 2),
        reduced_inverse,
    )


def solution(mesh):
    return jax.shard_map(
        shards,
        mesh=mesh,
        in_specs=(
            P(("dom", "grp"), None, None),
            P(("dom", "grp"), None, None),
            P(("dom", "grp"), None, None),
            P(("dom", "grp"), None),
            P(("dom", "grp")),
            P(("dom", "grp")),
            P(("dom", "grp"), None, None),
            P("dom", None, None),
        ),
        out_specs=P(("dom", "grp"), None, None),
        check_vma=False,
    )
```

```python
import functools

import jax
import jax.numpy as jnp
from jax import lax
from jax.experimental import pallas as pl
from jax.experimental.pallas import tpu as pltpu
from jax.sharding import PartitionSpec as P

CAP = 2
F32 = jnp.float32
BF16 = jnp.bfloat16


def partner(me, offset, count):
    other, bit = 0, 1
    while bit < count:
        other = other + ((me // bit + offset // bit) % 2) * bit
        bit *= 2
    return other


def chunks_of(start, stop, step):
    return [(low, min(low + step, stop)) for low in range(start, stop, step)]


def widen(rows, spread, blocks, depth):
    size = rows.shape[1]
    wide = jnp.dot(rows, spread[:size, : size * blocks], preferred_element_type=F32)
    row = lax.broadcasted_iota(jnp.int32, wide.shape, 0) // depth
    column = lax.broadcasted_iota(jnp.int32, wide.shape, 1) % blocks
    return jnp.where(row == column, wide, 0.0).astype(BF16)


def block_rows(weights, low, high, left, right):
    value = weights[low:high, :, left:right]
    return value.reshape((high - low) * weights.shape[1], right - left)


def kernel(
    regions,
    groups,
    region_ref,
    source_ref,
    target_ref,
    residual_hbm,
    binv_hbm,
    coupling_hbm,
    basis_hbm,
    rinv_hbm,
    second,
    solved,
    binv,
    coupling,
    basis,
    basis_t,
    residual,
    rinv,
    initial,
    gathered,
    wide,
    spread,
    total,
    products,
    corrected,
    send,
    recv,
    meta_send,
    meta_recv,
    red_send,
    red_recv,
    perm,
    meta_smem,
    load_sem,
    binv_sem,
    coupling_sem,
    send_sem,
    recv_sem,
    meta_send_sem,
    meta_recv_sem,
    meta_local_sem,
    red_send_sem,
    red_recv_sem,
):
    dom, grp = lax.axis_index("dom"), lax.axis_index("grp")
    elements, vectors, width = initial.shape
    tiles = products[0].shape[0]
    parts, blocks = coupling.shape[0], coupling.shape[2]
    modes = basis_t.shape[1]
    step = spread.shape[0]
    chunks = chunks_of(0, width, step)
    pieces = chunks_of(0, width, products[0].shape[2])

    load_residual = pltpu.make_async_copy(residual_hbm, residual, load_sem.at[0])
    load_basis = pltpu.make_async_copy(basis_hbm, basis_t, load_sem.at[1])
    load_rinv = pltpu.make_async_copy(rinv_hbm.at[0], rinv, load_sem.at[2])

    def load_binv(i):
        low, high = chunks[i]
        rows = pl.ds(low, high - low)
        return pltpu.make_async_copy(binv_hbm.at[rows], binv.at[rows], binv_sem.at[i])

    def load_coupling(h, i):
        low, high = chunks[i]
        rows = pl.ds(low, high - low)
        return pltpu.make_async_copy(
            coupling_hbm.at[rows, h], coupling.at[h, rows], coupling_sem.at[h, i]
        )

    load_residual.start()
    for i in range(len(chunks)):
        load_binv(i).start()
    for h in range(parts):
        for i in range(len(chunks)):
            load_coupling(h, i).start()
    load_basis.start()
    load_rinv.start()

    barrier = pltpu.get_barrier_semaphore()
    for k in range(1, regions):
        pl.semaphore_signal(barrier, inc=1, device_id=(partner(dom, k, regions), grp))
    for j in range(1, groups):
        pl.semaphore_signal(barrier, inc=1, device_id=(dom, partner(grp, j, groups)))

    row = lax.broadcasted_iota(jnp.int32, spread.shape, 0)
    column = lax.broadcasted_iota(jnp.int32, spread.shape, 1) // blocks
    spread[...] = jnp.where(row == column, 1.0, 0.0).astype(BF16)

    named = [region_ref[t] for t in range(tiles)]
    for k in range(regions):
        place = partner(dom, k, regions)
        first, last = jnp.int32(tiles), jnp.int32(-1)
        for t in range(tiles):
            last = jnp.where(named[t] == place, t, last)
            first = jnp.where(named[tiles - 1 - t] == place, tiles - 1 - t, first)
        has_first = last >= 0
        has_last = last > first
        first = jnp.where(has_first, first, 0)
        last = jnp.where(has_last, last, 0)
        perm[CAP * k] = first
        perm[CAP * k + 1] = last
        aim_first = jnp.where(has_first, target_ref[first], -1)
        aim_last = jnp.where(has_last, target_ref[last], -1)
        meta_send[k, 0:1, :] = jnp.full((1, 128), aim_first, jnp.int32)
        meta_send[k, 1:2, :] = jnp.full((1, 128), aim_last, jnp.int32)

    load_residual.wait()

    def rows_of(e):
        return pl.ds(e * vectors, vectors)

    for i, (low, high) in enumerate(chunks):
        value = widen(residual[:, low:high], spread, blocks, vectors)
        load_binv(i).wait()
        part = jnp.dot(
            value, block_rows(binv, low, high, 0, width), preferred_element_type=F32
        )
        if i == 0:
            total[...] = part
        else:
            total[...] += part
    for e in range(elements):
        initial[e] = total[rows_of(e)].astype(BF16)

    def meta_copy(k):
        return pltpu.make_async_remote_copy(
            src_ref=meta_send.at[k],
            dst_ref=meta_recv.at[k],
            send_sem=meta_send_sem.at[k],
            recv_sem=meta_recv_sem.at[k],
            device_id=(partner(dom, k, regions), grp),
        )

    pl.semaphore_wait(barrier, regions - 1 + groups - 1)
    for k in range(1, regions):
        meta_copy(k).start()
    meta_recv[0] = meta_send[0]

    for t in range(tiles):
        gathered[rows_of(t)] = initial[source_ref[t]]
    for h in range(parts):
        for low, high in chunks:
            wide[h, :, low * blocks : high * blocks] = widen(
                gathered[h * blocks * vectors : (h + 1) * blocks * vectors, low:high],
                spread,
                blocks,
                vectors,
            )

    def product_copy(p, k, c):
        s = CAP * k + c
        return pltpu.make_async_remote_copy(
            src_ref=send[p].at[s],
            dst_ref=recv[p].at[s],
            send_sem=send_sem.at[p, s],
            recv_sem=recv_sem.at[p, s],
            device_id=(partner(dom, k, regions), grp),
        )

    for p, (left, right) in enumerate(pieces):
        for h in range(parts):
            for i, (low, high) in enumerate(chunks):
                if p == 0:
                    load_coupling(h, i).wait()
                part = jnp.dot(
                    wide[h, :, low * blocks : high * blocks],
                    block_rows(coupling.at[h], low, high, left, right),
                    preferred_element_type=F32,
                )
                if i == 0:
                    total[:, left:right] = part
                else:
                    total[:, left:right] += part
            for i in range(blocks):
                products[p][h * blocks + i] = total[rows_of(i), left:right].astype(BF16)

        def send_products(i, carry, p=p):
            k = regions - 1 - i
            for c in range(CAP):
                send[p][CAP * k + c] = products[p][perm[CAP * k + c]]
                product_copy(p, k, c).start()
            return carry

        lax.fori_loop(0, regions - 1, send_products, 0)
        for c in range(CAP):
            recv[p][c] = products[p][perm[c]]

    load_basis.wait()
    load_rinv.wait()
    for e in range(elements):
        basis[e] = jnp.swapaxes(basis_t[e].astype(F32), 0, 1).astype(BF16)
    for k in range(1, regions):
        meta_copy(k).wait()
    meta_local = pltpu.make_async_copy(meta_recv, meta_smem, meta_local_sem.at[0])
    meta_local.start()
    meta_local.wait()

    for p, (left, right) in enumerate(pieces):

        def arrive(k, carry, p=p):
            for c in range(CAP):
                product_copy(p, k, c).wait_recv()
            return carry

        lax.fori_loop(1, regions, arrive, 0)

        def correct(e, carry, p=p):
            value = corrected[p][e].astype(F32)
            for k in range(regions):
                for c in range(CAP):
                    weight = jnp.where(meta_smem[k, c, 0] == e, 1.0, 0.0).astype(F32)
                    value = value - weight * recv[p][CAP * k + c].astype(F32)
            corrected[p][e] = value.astype(BF16)
            return carry

        for e in range(elements):
            corrected[p][e] = residual[rows_of(e), left:right]
        lax.fori_loop(0, elements, correct, 0)
        rows = corrected[p][...].reshape(elements * vectors, right - left)
        for low, high in chunks_of(left, right, step):
            part = jnp.dot(
                widen(rows[:, low - left : high - left], spread, blocks, vectors),
                block_rows(binv, low, high, 0, width),
                preferred_element_type=F32,
            )
            if low == 0:
                total[...] = part
            else:
                total[...] += part

    reduced = jnp.zeros((vectors, modes), F32)
    for e in range(elements):
        value = total[rows_of(e)]
        second[e] = value
        reduced = reduced + jnp.dot(
            value.astype(BF16), basis[e], preferred_element_type=F32
        )
    red_send[...] = reduced

    def red_copy(j):
        return pltpu.make_async_remote_copy(
            src_ref=red_send,
            dst_ref=red_recv.at[j - 1],
            send_sem=red_send_sem.at[j - 1],
            recv_sem=red_recv_sem.at[j - 1],
            device_id=(dom, partner(grp, j, groups)),
        )

    for j in range(1, groups):
        red_copy(j).start()
    for p in range(len(pieces)):
        for k in range(1, regions):
            for c in range(CAP):
                product_copy(p, k, c).wait_send()
    for j in range(1, groups):
        red_copy(j).wait()
        reduced = reduced + red_recv[j - 1]
    solved[...] = jnp.dot(
        reduced, rinv[...], precision=lax.Precision.HIGHEST, preferred_element_type=F32
    ).astype(BF16)


def shards(
    residual_in,
    block_inverse,
    coupling,
    tile_region,
    tile_source,
    tile_target,
    interface_basis,
    reduced_inverse,
):
    regions, groups = lax.axis_size("dom"), lax.axis_size("grp")
    elements, vectors, width = residual_in.shape
    tiles = coupling.shape[0]
    modes = interface_basis.shape[2]
    slots = regions * CAP
    parts = tiles // elements
    step = 128
    chunks = len(chunks_of(0, width, step))
    pieces = [high - low for low, high in chunks_of(0, width, 2 * step)]
    smem = pl.BlockSpec(memory_space=pltpu.SMEM)
    vmem = pl.BlockSpec(memory_space=pltpu.VMEM)
    hbm = pl.BlockSpec(memory_space=pl.ANY)
    dma = pltpu.SemaphoreType.DMA
    second, solved = pl.pallas_call(
        functools.partial(kernel, regions, groups),
        out_shape=(
            jax.ShapeDtypeStruct((elements, vectors, width), F32),
            jax.ShapeDtypeStruct((vectors, modes), BF16),
        ),
        in_specs=[smem] * 3 + [hbm] * 5,
        out_specs=(vmem, vmem),
        scratch_shapes=[
            pltpu.VMEM((width, elements, width), BF16),
            pltpu.VMEM((parts, width, elements, width), BF16),
            pltpu.VMEM((elements, width, modes), BF16),
            pltpu.VMEM((elements, modes, width), BF16),
            pltpu.VMEM((elements * vectors, width), BF16),
            pltpu.VMEM((modes, modes), F32),
            pltpu.VMEM((elements, vectors, width), BF16),
            pltpu.VMEM((tiles * vectors, width), BF16),
            pltpu.VMEM((parts, elements * vectors, width * elements), BF16),
            pltpu.VMEM((step, step * elements), BF16),
            pltpu.VMEM((elements * vectors, width), F32),
            [pltpu.VMEM((tiles, vectors, size), BF16) for size in pieces],
            [pltpu.VMEM((elements, vectors, size), BF16) for size in pieces],
            [pltpu.VMEM((slots, vectors, size), BF16) for size in pieces],
            [pltpu.VMEM((slots, vectors, size), BF16) for size in pieces],
            pltpu.VMEM((regions, 8, 128), jnp.int32),
            pltpu.VMEM((regions, 8, 128), jnp.int32),
            pltpu.VMEM((vectors, modes), F32),
            pltpu.VMEM((groups - 1, vectors, modes), F32),
            pltpu.SMEM((slots,), jnp.int32),
            pltpu.SMEM((regions, 8, 128), jnp.int32),
            dma((3,)),
            dma((chunks,)),
            dma((parts, chunks)),
            dma((len(pieces), slots)),
            dma((len(pieces), slots)),
            dma((regions,)),
            dma((regions,)),
            dma((1,)),
            dma((groups - 1,)),
            dma((groups - 1,)),
        ],
        compiler_params=pltpu.CompilerParams(
            collective_id=0, has_side_effects=True, vmem_limit_bytes=56 * 1024 * 1024
        ),
        cost_estimate=pl.CostEstimate(
            flops=2 * vectors * width * width * (2 * elements + tiles),
            bytes_accessed=2 * width * width * (elements + tiles),
            transcendentals=0,
        ),
    )(
        tile_region[:, 0],
        tile_source,
        tile_target,
        residual_in.reshape(elements * vectors, width),
        jnp.transpose(block_inverse, (1, 0, 2)),
        jnp.transpose(coupling, (1, 0, 2)).reshape(width, parts, elements, width),
        jnp.swapaxes(interface_basis, 1, 2),
        reduced_inverse,
    )
    correction = jnp.einsum("km,ebm->ekb", solved, interface_basis, preferred_element_type=F32)
    return second + correction


def solution(mesh):
    return jax.shard_map(
        shards,
        mesh=mesh,
        in_specs=(
            P(("dom", "grp"), None, None),
            P(("dom", "grp"), None, None),
            P(("dom", "grp"), None, None),
            P(("dom", "grp"), None),
            P(("dom", "grp")),
            P(("dom", "grp")),
            P(("dom", "grp"), None, None),
            P("dom", None, None),
        ),
        out_specs=P(("dom", "grp"), None, None),
        check_vma=False,
    )
```
